128 devices in a mesh: seq: 16 (over x, z), head: 8 (over y, core).
Axes of the slice: x: 4, y: 4, z: 4, core: 2. Of those that a mesh axis runs over, the one named last changes fastest.
Arguments:
- tokens: bfloat16 [8192, 8192], P('seq'), may hold values from -6 to 6
- w_query: bfloat16 [8192, 8192], P(None, 'head'), may hold values from -0.0625 to 0.0625
- w_key: bfloat16 [8192, 1024], P(None, 'head'), may hold values from -0.0625 to 0.0625
- w_value: bfloat16 [8192, 1024], P(None, 'head'), may hold values from -0.0625 to 0.0625
- b_query: bfloat16 [8192], P('head'), may hold values from -3 to 3
- b_key: bfloat16 [1024], P('head'), may hold values from -3 to 3
- b_value: bfloat16 [1024], P('head'), may hold values from -3 to 3
- prefix_keys: bfloat16 [16, 256, 1024], P('seq', None, 'head'), may hold values from -420 to 420
- prefix_values: bfloat16 [16, 256, 1024], P('seq', None, 'head'), may hold values from -6 to 6
- decode_rows: bfloat16 [64, 4, 8192], P('seq', None, 'head'), may hold values from -6 to 6
- page_table: int32 [64], replicated, may hold values from 0 to 63, as said below
- prompt_len: int32 [64], replicated, may hold values from 1 to 128
- soft_ids: int32 [64], replicated, may hold values from 0 to 15
- plan: int32 [128], replicated, may hold values from -1 to 63, as said below
Outputs:
- prefill_out: bfloat16 [8192, 8192], P('seq', 'head')
- decode_out: bfloat16 [128, 4, 8192], P('seq', None, 'head')
The draws below stay inside these ranges and needn't reach their ends.
Inputs may be any that keep to these rules, and one draw needn't show every extreme that they name: `page_table`: the page of request r is one of pages 4 * (r // 4) to 4 * (r // 4) + 3; every page belongs to exactly one request. `plan`: every request stands in exactly one slot; no owner receives two requests of one block of 4 consecutive requests; some owner has all 8 slots used.
All inputs are finite; a program needn't handle non-finite values.
Results may differ from the reference program's by a relative error of at most 0.018.
Values may be sent and summed in bfloat16 or wider, within the bound.
A program may use at most 128 MiB of HBM per device.

```python
import math
import jax
import jax.numpy as jnp
from jax import lax

D = 8192
KVH = 8
HD = 128
PAGE = 128
PFX_LEN = 256
STEPS = 4
TOK_DEV = 512
QH = 64
REQ_DEV = 4
REQS = 64
TOKENS = 8192
R_CAP = 8
OWN_SLOTS = 128
NPFX = 16
N_SEQ = 16


def draw_prefix_keys(key, part):
    key = jax.random.fold_in(key, 11)
    full_shape = (NPFX, PFX_LEN, KVH * HD)
    return jax.random.normal(key, full_shape, jnp.float32).astype(jnp.bfloat16)


def draw_page_table(key, part):
    key = jax.random.fold_in(key, 23)
    senders = REQS // REQ_DEV
    subkeys = jax.random.split(key, senders)
    orders = jax.vmap(lambda sub: jax.random.permutation(sub, REQ_DEV))(subkeys).astype(jnp.int32)
    block_base = jnp.arange(senders, dtype=jnp.int32)[:, None] * REQ_DEV
    return (orders + block_base).reshape(REQS)


def draw_prompt_len(key, part):
    key = jax.random.fold_in(key, 37)
    drawn_len = jax.random.randint(key, (REQS,), 1, PAGE + 1)
    full_at = jax.random.randint(jax.random.fold_in(key, 1), (), 0, REQS)
    return jnp.where(jnp.arange(REQS) == full_at, PAGE, drawn_len).astype(jnp.int32)


def draw_plan(key, part):
    key = jax.random.fold_in(key, 41)
    senders = REQS // REQ_DEV
    owners_perm = jax.random.permutation(key, senders).astype(jnp.int32)
    subkeys = jax.random.split(jax.random.fold_in(key, 1), senders)
    offsets = jax.vmap(lambda sub: jax.random.permutation(sub, REQ_DEV))(subkeys).astype(jnp.int32)
    sender = jnp.arange(senders, dtype=jnp.int32)[:, None]
    owner_of = owners_perm[(sender // 2 + offsets) % senders].reshape(REQS)
    order_key = jax.random.permutation(jax.random.fold_in(key, 2), REQS).astype(jnp.int32)
    same_owner = owner_of[:, None] == owner_of[None, :]
    earlier = order_key[None, :] < order_key[:, None]
    rank_in = jnp.sum(same_owner & earlier, axis=1).astype(jnp.int32)
    slot_keys = jax.random.split(jax.random.fold_in(key, 3), senders)
    slot_perm = jax.vmap(lambda sub: jax.random.permutation(sub, R_CAP))(slot_keys).astype(jnp.int32)
    slot_of = owner_of * R_CAP + slot_perm[owner_of, rank_in]
    slot_table = jnp.full((senders * R_CAP,), -1, jnp.int32)
    return slot_table.at[slot_of].set(jnp.arange(REQS, dtype=jnp.int32))


def touch_ends(result, stream_key, low, high):
    spot = [jax.random.randint(jax.random.fold_in(stream_key, axis), (), 0, length) for axis, length in enumerate(result.shape)]
    widest = result.shape.index(max(result.shape))
    neighbour = spot[:widest] + [(spot[widest] + 1) % result.shape[widest]] + spot[widest + 1:]
    return result.at[tuple(spot)].set(low).at[tuple(neighbour)].set(high)


def block_levels(rng, dims, shards, smallest, high):
    level, own = 1.0, jax.random.fold_in(rng, 6)
    for dim, blocks in shards:
        heights = jnp.exp(jax.random.uniform(jax.random.fold_in(own, dim), (blocks,), jnp.float32, smallest / len(shards), high / len(shards)))
        level = level * jnp.repeat(heights, dims[dim] // blocks).reshape([-1 if axis == dim else 1 for axis in range(len(dims))])
    return level


def gaussian(own_key, extent, width, limit, shards=(), kind=jnp.bfloat16):
    entries = jax.random.normal(own_key, extent, jnp.float32) * width
    if len(shards) > 0:
        entries = block_levels(own_key, extent, shards, -0.22, 0.18) * entries
    return jnp.clip(entries, min=-limit, max=limit).astype(kind)


def setup_inputs(seed: int = 0) -> dict:
    key_of = jax.random.split(jax.random.key(seed), 15)
    return {
        "tokens": gaussian(key_of[0], (TOKENS, D), 1.0, 6.0, ((0, 16),)),
        "w_query": gaussian(key_of[1], (D, QH * HD), D ** -0.5, 0.0625, ((1, 8),)),
        "w_key": gaussian(key_of[2], (D, KVH * HD), D ** -0.5, 0.0625, ((1, 8),)),
        "w_value": gaussian(key_of[3], (D, KVH * HD), D ** -0.5, 0.0625, ((1, 8),)),
        "b_query": gaussian(key_of[4], (QH * HD,), 0.5, 3.0, ((0, 8),)),
        "b_key": gaussian(key_of[5], (KVH * HD,), 0.5, 3.0, ((0, 8),)),
        "b_value": gaussian(key_of[6], (KVH * HD,), 0.5, 3.0, ((0, 8),)),
        "prefix_keys": draw_prefix_keys(jax.random.fold_in(key_of[14], 71), 0),
        "prefix_values": gaussian(key_of[8], (NPFX, PFX_LEN, KVH * HD), 1.0, 6.0, ((0, 16), (2, 8))),
        "decode_rows": gaussian(key_of[9], (REQS, STEPS, D), 1.0, 6.0, ((0, 16), (2, 8))),
        "page_table": draw_page_table(jax.random.fold_in(key_of[14], 71), 0),
        "prompt_len": draw_prompt_len(jax.random.fold_in(key_of[14], 71), 0),
        "soft_ids": touch_ends(jax.random.randint(key_of[12], (REQS,), 0, NPFX), jax.random.fold_in(key_of[12], 1), 0, NPFX - 1).astype(jnp.int32),
        "plan": draw_plan(jax.random.fold_in(key_of[14], 71), 0),
    }


rope_theta = 1000000.0

def rotate(vectors, positions):
    half_dim = vectors.shape[-1] // 2
    frequency = rope_theta ** (-jnp.arange(half_dim, dtype=jnp.float32) * 2.0 / vectors.shape[-1])
    angles = positions.astype(jnp.float32)[..., None, None] * frequency
    cosine = jnp.cos(angles)
    sine_part = jnp.sin(angles)
    first_half = vectors[..., :half_dim]
    second = vectors[..., half_dim:]
    return jnp.concatenate([first_half * cosine - second * sine_part, second * cosine + first_half * sine_part], axis=-1)

def project(row_block, weight, bias_vec):
    return jnp.dot(row_block, weight, preferred_element_type=jnp.float32) + bias_vec.astype(jnp.float32)

def attend(queries, key_rows, value_rows, key_mask):
    inv_scale = 1.0 / math.sqrt(queries.shape[-1])
    scores = jnp.einsum('brcgd,bscd->bcgrs', queries.astype(jnp.float32), key_rows.astype(jnp.float32)) * inv_scale
    scores = jnp.where(key_mask[:, None, None], scores, -jnp.inf)
    row_max = lax.optimization_barrier(jnp.max(scores, axis=-1, keepdims=True))
    exponent = jnp.exp(scores - row_max)
    weights = (exponent / lax.optimization_barrier(jnp.sum(exponent, axis=-1, keepdims=True))).astype(jnp.bfloat16)
    return jnp.einsum('bcgrs,bscd->brcgd', weights.astype(jnp.float32), value_rows.astype(jnp.float32))

def prefill(row_block, live_len, soft_pick, query_w, key_w, value_w, query_b, key_b, value_b, table_keys, table_values):
    page_count = live_len.shape[0]
    page_size = row_block.shape[0] // page_count
    kv_heads = key_w.shape[1] // HD
    groups = query_w.shape[1] // key_w.shape[1]
    offsets = jnp.arange(page_size, dtype=jnp.int32)
    live_mask = offsets[None, :] < live_len[:, None]
    positions = table_keys.shape[1] + jnp.broadcast_to(offsets[None, :], live_mask.shape)
    queries = rotate(project(row_block, query_w, query_b).reshape(page_count, page_size, kv_heads * groups, HD), positions)
    queries = queries.astype(jnp.bfloat16).reshape(page_count, page_size, kv_heads, groups, HD)
    key_rows = rotate(project(row_block, key_w, key_b).reshape(page_count, page_size, kv_heads, HD), positions)
    key_rows = (key_rows * live_mask[:, :, None, None]).astype(jnp.bfloat16)
    value_rows = project(row_block, value_w, value_b).reshape(page_count, page_size, kv_heads, HD)
    value_rows = (value_rows * live_mask[:, :, None, None]).astype(jnp.bfloat16)
    prefix_size = table_keys.shape[1]
    fixed_keys = jnp.take(table_keys, soft_pick, axis=0).reshape(page_count, prefix_size, kv_heads, HD)
    fixed_values = jnp.take(table_values, soft_pick, axis=0).reshape(page_count, prefix_size, kv_heads, HD)
    causal = (offsets[None, :] <= offsets[:, None])[None] & live_mask[:, None, :]
    key_mask = jnp.concatenate([jnp.ones((page_count, page_size, prefix_size), jnp.bool_), causal], axis=2)
    attended = attend(queries, jnp.concatenate([fixed_keys, key_rows], axis=1), jnp.concatenate([fixed_values, value_rows], axis=1), key_mask)
    attended = (attended * live_mask[:, :, None, None, None]).astype(jnp.bfloat16)
    return (attended.reshape(page_count * page_size, kv_heads * groups * HD), key_rows, value_rows)

def decode(row_block, live_len, soft_pick, prompt_keys, prompt_values, query_w, key_w, value_w, query_b, key_b, value_b, table_keys, table_values):
    slot_count = row_block.shape[0]
    step_count = row_block.shape[1]
    kv_heads = key_w.shape[1] // HD
    groups = query_w.shape[1] // key_w.shape[1]
    flat_rows = row_block.reshape(slot_count * step_count, row_block.shape[2])
    prefix_size = table_keys.shape[1]
    step_ids = jnp.arange(step_count, dtype=jnp.int32)
    positions = prefix_size + live_len[:, None] + step_ids[None, :]
    queries = rotate(project(flat_rows, query_w, query_b).reshape(slot_count, step_count, kv_heads * groups, HD), positions)
    queries = queries.astype(jnp.bfloat16).reshape(slot_count, step_count, kv_heads, groups, HD)
    key_rows = rotate(project(flat_rows, key_w, key_b).reshape(slot_count, step_count, kv_heads, HD), positions).astype(jnp.bfloat16)
    value_rows = project(flat_rows, value_w, value_b).reshape(slot_count, step_count, kv_heads, HD).astype(jnp.bfloat16)
    page_size = prompt_keys.shape[1]
    fixed_keys = jnp.take(table_keys, soft_pick, axis=0).reshape(slot_count, prefix_size, kv_heads, HD)
    fixed_values = jnp.take(table_values, soft_pick, axis=0).reshape(slot_count, prefix_size, kv_heads, HD)
    prompt_live = jnp.arange(page_size, dtype=jnp.int32)[None, :] < live_len[:, None]
    causal = step_ids[None, :] <= step_ids[:, None]
    key_mask = jnp.concatenate([jnp.ones((slot_count, step_count, prefix_size), jnp.bool_), jnp.broadcast_to(prompt_live[:, None, :], (slot_count, step_count, page_size)), jnp.broadcast_to(causal[None], (slot_count, step_count, step_count))], axis=2)
    all_keys = jnp.concatenate([fixed_keys, prompt_keys, key_rows], axis=1)
    all_values = jnp.concatenate([fixed_values, prompt_values, value_rows], axis=1)
    return attend(queries, all_keys, all_values, key_mask)

def reference(tokens, w_query, w_key, w_value, b_query, b_key, b_value, prefix_keys, prefix_values, decode_rows, page_table, prompt_len, soft_ids, plan):
    page_owner = jnp.zeros((REQS,), jnp.int32).at[page_table].set(jnp.arange(REQS, dtype=jnp.int32))
    page_len = prompt_len[page_owner]
    page_soft = soft_ids[page_owner]

    def one_block(block):
        return prefill(block[0], block[1], block[2], w_query, w_key, w_value, b_query, b_key, b_value, prefix_keys, prefix_values)
    attended, key_pages, value_pages = lax.map(one_block, (tokens.reshape(N_SEQ, TOK_DEV, D), page_len.reshape(N_SEQ, REQ_DEV), page_soft.reshape(N_SEQ, REQ_DEV)))
    prefill_out = attended.reshape(TOKENS, QH * HD)
    key_pages = key_pages.reshape((REQS,) + key_pages.shape[2:])
    value_pages = value_pages.reshape((REQS,) + value_pages.shape[2:])
    live_slot = plan >= 0
    wanted = jnp.maximum(plan, 0)
    their_pages = page_table[wanted]
    decoded = decode(decode_rows[wanted], prompt_len[wanted], soft_ids[wanted], key_pages[their_pages], value_pages[their_pages], w_query, w_key, w_value, b_query, b_key, b_value, prefix_keys, prefix_values)
    decode_out = (decoded * live_slot[:, None, None, None, None]).astype(jnp.bfloat16).reshape(OWN_SLOTS, STEPS, QH * HD)
    return (prefill_out, decode_out)
```

```python
import functools
import math

import jax
import jax.numpy as jnp
import numpy as np
from jax import lax
from jax.experimental import pallas as pl
from jax.experimental.pallas import tpu as pltpu
from jax.sharding import PartitionSpec as P

HD = 128
PAGE = 128
PFX = 256
STEPS = 4
REQ = 4
SLOTS = 8
NS = 16
NH = 8
GROUP = 8
D = 8192
TOK = REQ * PAGE
ROWS = TOK + REQ * STEPS
QW = GROUP * HD
W = QW + 2 * HD
KC = 512
NC = D // KC
PER = NC // NH
LOOK = 4
PIECE = PFX // NS
HEADS_AT_ONCE = 2
MESH = pl.DeviceIdType.MESH
EXP2_SCALE = math.log2(math.e) / math.sqrt(HD)
ROPE_ROWS = 136


def rope_table():
    frequency = 1000000.0 ** (-np.arange(HD // 2, dtype=np.float64) * 2.0 / HD)
    angles = (PFX + np.arange(ROPE_ROWS, dtype=np.float64))[:, None] * frequency
    cosine = np.concatenate([np.cos(angles), np.cos(angles)], axis=1)
    sine = np.concatenate([-np.sin(angles), np.sin(angles)], axis=1)
    return np.stack([cosine, sine]).astype(np.float32)


def rotate(vectors, cosine, sine):
    return vectors * cosine + pltpu.roll(vectors, HD // 2, 1) * sine


def scores_of(queries, keys):
    return lax.dot_general(queries, keys, (((1,), (1,)), ((), ())), preferred_element_type=jnp.float32)


def kernel(
    tokens, w_query, w_key, w_value, b_query, b_key, b_value, prefix_keys, prefix_values, decode_rows,
    page_table, prompt_len, soft_ids, plan, rope,
    prefill_out, decode_out,
    x, w, acc, queries, keys, values, key_all, value_all, out_stage,
    bq, bk, bv, rope_v, drows, drow_stage, piece, dealt, picked, prefix, dq, dk, dv, dec_keys, dec_values, dec_f32,
    dec_res, dec_send, dec_recv, dec_out_v,
    table_s, len_s, soft_s, plan_s,
    chunk_sem, small_sem, out_sem, rows_send, rows_recv, deal_send, deal_recv, pick_send, pick_recv, res_send, res_recv,
):
    s = lax.axis_index("seq")
    h = lax.axis_index("head")

    def chunk_copies(i):
        c = lax.rem(PER * h + i, NC)
        at = pl.ds(pl.multiple_of(c * KC, KC), KC)
        return (
            pltpu.make_async_copy(tokens.at[:, at], x.at[c, pl.ds(0, TOK), :], chunk_sem.at[0, c]),
            pltpu.make_async_copy(w_query.at[at, :], w.at[c, :, pl.ds(0, QW)], chunk_sem.at[1, c]),
            pltpu.make_async_copy(w_key.at[at, :], w.at[c, :, pl.ds(QW, HD)], chunk_sem.at[2, c]),
            pltpu.make_async_copy(w_value.at[at, :], w.at[c, :, pl.ds(QW + HD, HD)], chunk_sem.at[3, c]),
        )

    small = [
        pltpu.make_async_copy(src, dst, small_sem.at[n])
        for n, (src, dst) in enumerate(
            (
                (prefix_keys, piece.at[:, pl.ds(0, PIECE), :]),
                (prefix_values, piece.at[:, pl.ds(PIECE, PIECE), :]),
                (decode_rows, drows),
                (page_table, table_s),
                (prompt_len, len_s),
                (soft_ids, soft_s),
                (plan, plan_s),
                (b_query, bq),
                (b_key, bk),
                (b_value, bv),
                (rope, rope_v),
            )
        )
    ]

    barrier = pltpu.get_barrier_semaphore()

    def greet_seq(k, _):
        pl.semaphore_signal(barrier, inc=1, device_id=(lax.rem(s + k, NS), h), device_id_type=MESH)
        return 0

    def greet_head(k, _):
        pl.semaphore_signal(barrier, inc=1, device_id=(s, lax.rem(h + k, NH)), device_id_type=MESH)
        return 0

    lax.fori_loop(1, NS, greet_seq, 0)
    lax.fori_loop(1, NH, greet_head, 0)
    for copy in small[:3]:
        copy.start()
    for i in range(LOOK):
        for copy in chunk_copies(i):
            copy.start()
    for copy in small[3:]:
        copy.start()
    acc[...] = jnp.zeros_like(acc)

    for copy in small[:3]:
        copy.wait()
    own_rows = jnp.concatenate([drows[i].astype(jnp.float32) for i in range(REQ)], axis=0).astype(jnp.bfloat16)
    for n in range(PER):
        drow_stage[n] = own_rows[:, n * KC : (n + 1) * KC]
        x[PER * h + n, TOK:ROWS, :] = own_rows[:, n * KC : (n + 1) * KC]
    dealt[s] = piece[s]
    pl.semaphore_wait(barrier, NS - 1 + NH - 1)

    def rows_copy(peer, owner, k):
        return pltpu.make_async_remote_copy(
            src_ref=drow_stage,
            dst_ref=x.at[pl.ds(PER * owner, PER), pl.ds(TOK, ROWS - TOK), :],
            send_sem=rows_send.at[k],
            recv_sem=rows_recv.at[owner],
            device_id=(s, peer),
            device_id_type=MESH,
        )

    def deal_copy(peer, owner):
        return pltpu.make_async_remote_copy(
            src_ref=piece.at[peer],
            dst_ref=dealt.at[owner],
            send_sem=deal_send.at[peer],
            recv_sem=deal_recv.at[owner],
            device_id=(peer, h),
            device_id_type=MESH,
        )

    def pick_copy(peer, owner):
        return pltpu.make_async_remote_copy(
            src_ref=picked.at[peer],
            dst_ref=prefix.at[owner],
            send_sem=pick_send.at[peer],
            recv_sem=pick_recv.at[owner],
            device_id=(peer, h),
            device_id_type=MESH,
        )

    def result_copy(peer, owner):
        return pltpu.make_async_remote_copy(
            src_ref=dec_send.at[peer],
            dst_ref=dec_recv.at[owner],
            send_sem=res_send.at[peer],
            recv_sem=res_recv.at[owner],
            device_id=(peer, h),
            device_id_type=MESH,
        )

    def over_seq(act):
        def step(k, _):
            act(lax.rem(s + k, NS))
            return 0

        lax.fori_loop(1, NS, step, 0)

    def send_rows(k, _):
        rows_copy(lax.rem(h + NH - k, NH), h, k).start()
        return 0

    over_seq(lambda peer: deal_copy(peer, s).start())
    lax.fori_loop(1, NH, send_rows, 0)

    def pick():
        over_seq(lambda peer: deal_copy(s, peer).wait_recv())

        def one(d, _):
            for j in range(REQ):
                picked[d, j] = dealt[soft_s[REQ * d + j]]
            return 0

        lax.fori_loop(0, NS, one, 0)
        prefix[s] = picked[s]
        over_seq(lambda peer: pick_copy(peer, s).start())

    def project(i, _):
        c = lax.rem(PER * h + i, NC)
        for copy in chunk_copies(i):
            copy.wait()

        @pl.when(jnp.logical_and(lax.rem(i, PER) == 0, i > 0))
        def _():
            owner = lax.rem(h + i // PER, NH)
            rows_copy(h, owner, 0).wait_recv()

        @pl.when(i < NC - LOOK)
        def _():
            for copy in chunk_copies(i + LOOK):
                copy.start()

        @pl.when(i == 5)
        def _():
            pick()

        for n in range(W // 256):
            at = slice(256 * n, 256 * n + 256)
            acc[:, at] += jnp.dot(x[c], w[c, :, at], preferred_element_type=jnp.float32)
        return 0

    for copy in small[3:]:
        copy.wait()
    lax.fori_loop(0, NC, project, 0)

    row_in_block = lax.broadcasted_iota(jnp.int32, (REQ * STEPS, HD), 0)
    cosine_d = jnp.concatenate([rope_v[0, pl.ds(len_s[REQ * s + i], STEPS), :] for i in range(REQ)], axis=0)
    sine_d = jnp.concatenate([rope_v[1, pl.ds(len_s[REQ * s + i], STEPS), :] for i in range(REQ)], axis=0)
    b_q = bq[...].astype(jnp.float32).reshape(1, QW)
    b_k = bk[...].astype(jnp.float32).reshape(1, HD)
    b_v = bv[...].astype(jnp.float32).reshape(1, HD)
    for j in range(GROUP):
        at = slice(HD * j, HD * j + HD)
        rotated = rotate(acc[TOK:ROWS, at] + b_q[:, at], cosine_d, sine_d)
        dec_f32[...] = rotated
        for i in range(REQ):
            dq[i, STEPS * j : STEPS * j + STEPS, :] = dec_f32[STEPS * i : STEPS * i + STEPS, :]
    dk[...] = rotate(acc[TOK:ROWS, QW : QW + HD] + b_k, cosine_d, sine_d).astype(jnp.bfloat16)
    dv[...] = (acc[TOK:ROWS, QW + HD : W] + b_v).astype(jnp.bfloat16)

    cosine = rope_v[0, 0:PAGE, :]
    sine = rope_v[1, 0:PAGE, :]

    def finish(p, _):
        rows = pl.ds(pl.multiple_of(p * PAGE, PAGE), PAGE)
        keys[p] = rotate(acc[rows, QW : QW + HD] + b_k, cosine, sine).astype(jnp.bfloat16)
        values[p] = (acc[rows, QW + HD : W] + b_v).astype(jnp.bfloat16)
        for j in range(GROUP):
            at = slice(HD * j, HD * j + HD)
            queries[p, HD * j : HD * j + HD, :] = rotate(acc[rows, at] + b_q[:, at], cosine, sine).astype(jnp.bfloat16)
        return 0

    lax.fori_loop(0, REQ, finish, 0)
    over_seq(lambda peer: pick_copy(s, peer).wait_recv())

    ones = jnp.ones((PFX + 2 * PAGE, HD), jnp.bfloat16)
    value_all[:, HD:] = ones
    col = lax.broadcasted_iota(jnp.int32, (GROUP * STEPS, PFX + 2 * PAGE), 1)
    row = lax.broadcasted_iota(jnp.int32, (GROUP * STEPS, PFX + 2 * PAGE), 0)
    for i in range(REQ):
        page = jnp.clip(table_s[REQ * s + i] - REQ * s, 0, REQ - 1)
        key_all[0:PFX, :] = prefix[:, i, 0:PIECE, :].reshape(PFX, HD)
        value_all[0:PFX, 0:HD] = prefix[:, i, PIECE : 2 * PIECE, :].reshape(PFX, HD)
        key_all[PFX : PFX + PAGE, :] = keys[page]
        value_all[PFX : PFX + PAGE, 0:HD] = values[page]
        key_all[PFX + PAGE : PFX + PAGE + REQ * STEPS, :] = dk[...]
        value_all[PFX + PAGE : PFX + PAGE + REQ * STEPS, 0:HD] = dv[...]
        if i == 0:
            empty = PFX + PAGE + REQ * STEPS
            key_all[empty:, :] = jnp.zeros((PFX + 2 * PAGE - empty, HD), jnp.bfloat16)
            value_all[empty:, 0:HD] = jnp.zeros((PFX + 2 * PAGE - empty, HD), jnp.bfloat16)
        first = PFX + PAGE + STEPS * i
        live = (col < PFX + len_s[REQ * s + i]) | ((col >= first) & (col - first <= lax.rem(row, STEPS)))
        score = jnp.where(live, scores_of(dq[i].astype(jnp.bfloat16), key_all[...]), -1e30)
        weight = jnp.exp2((score - jnp.max(score, axis=1, keepdims=True)) * EXP2_SCALE).astype(jnp.bfloat16)
        total = jnp.dot(weight, value_all[...], preferred_element_type=jnp.float32)
        dec_res[i] = (total[:, 0:HD] / total[:, HD:]).astype(jnp.bfloat16)

    def route(o, _):
        which = 0
        for c in range(SLOTS):
            offset = plan_s[SLOTS * o + c] - REQ * s
            which += jnp.where((offset >= 0) & (offset < REQ), offset, 0)
        dec_send[o] = dec_res[jnp.minimum(which, REQ - 1)]
        return 0

    lax.fori_loop(0, NS, route, 0)
    dec_recv[s] = dec_send[s]
    over_seq(lambda peer: result_copy(peer, s).start())

    causal = jnp.where(
        lax.broadcasted_iota(jnp.int32, (PAGE, PAGE), 1) <= lax.broadcasted_iota(jnp.int32, (PAGE, PAGE), 0), 0.0, -1e30
    )
    causal = jnp.concatenate([causal] * HEADS_AT_ONCE, axis=0)
    slot = lax.broadcasted_iota(jnp.int32, (PAGE, HD), 0)

    def out_copy(p):
        rows = pl.ds(pl.multiple_of(p * PAGE, PAGE), PAGE)
        return pltpu.make_async_copy(out_stage.at[rows, :], prefill_out.at[rows, :], out_sem.at[p])

    def attend(p, _):
        rows = pl.ds(pl.multiple_of(p * PAGE, PAGE), PAGE)
        holder, length = 0, 0
        for i in range(REQ):
            mine = table_s[REQ * s + i] == REQ * s + p
            holder += jnp.where(mine, i, 0)
            length += jnp.where(mine, len_s[REQ * s + i], 0)
        holder = jnp.minimum(holder, REQ - 1)
        key_all[0:PFX, :] = prefix[:, holder, 0:PIECE, :].reshape(PFX, HD)
        value_all[0:PFX, 0:HD] = prefix[:, holder, PIECE : 2 * PIECE, :].reshape(PFX, HD)
        key_all[PFX : PFX + PAGE, :] = keys[p]
        value_all[PFX : PFX + PAGE, 0:HD] = values[p]
        for g in range(GROUP // HEADS_AT_ONCE):
            n = HEADS_AT_ONCE * HD
            query = queries[p, g * n : (g + 1) * n, :]
            score = scores_of(query, key_all[0 : PFX + PAGE, :])
            fixed, own = score[:, 0:PFX], score[:, PFX:] + causal
            top = jnp.maximum(jnp.max(fixed, axis=1, keepdims=True), jnp.max(own, axis=1, keepdims=True))
            fixed = jnp.exp2((fixed - top) * EXP2_SCALE).astype(jnp.bfloat16)
            own = jnp.exp2((own - top) * EXP2_SCALE).astype(jnp.bfloat16)
            total = jnp.dot(
                jnp.concatenate([fixed, own], axis=1), value_all[0 : PFX + PAGE, :], preferred_element_type=jnp.float32
            )
            result = total[:, 0:HD] / total[:, HD:]
            for j in range(HEADS_AT_ONCE):
                at = (g * HEADS_AT_ONCE + j) * HD
                out_stage[rows, at : at + HD] = jnp.where(
                    slot < length, result[HD * j : HD * j + HD, :], 0.0
                ).astype(jnp.bfloat16)
        out_copy(p).start()
        return 0

    lax.fori_loop(0, REQ, attend, 0)

    over_seq(lambda peer: result_copy(s, peer).wait_recv())
    for c in range(SLOTS):
        request = plan_s[SLOTS * s + c]
        live = jnp.where(request >= 0, 1.0, 0.0)
        dq[0] = dec_recv[jnp.maximum(request, 0) // REQ].astype(jnp.float32) * live
        dec_out_v[c] = jnp.concatenate(
            [dq[0, STEPS * j : STEPS * j + STEPS, :] for j in range(GROUP)], axis=1
        ).astype(jnp.bfloat16)
    done = pltpu.make_async_copy(dec_out_v, decode_out, small_sem.at[0])
    done.start()

    def drain(k, _):
        rows_copy(h, h, k).wait_send()
        return 0

    lax.fori_loop(1, NH, drain, 0)
    over_seq(lambda peer: deal_copy(peer, s).wait_send())
    over_seq(lambda peer: pick_copy(peer, s).wait_send())
    over_seq(lambda peer: result_copy(peer, s).wait_send())
    for p in range(REQ):
        out_copy(p).wait()
    done.wait()


def body(*operands):
    (tokens, w_query, w_key, w_value, b_query, b_key, b_value, prefix_keys, prefix_values, decode_rows, *tables) = operands
    bf16, f32, i32 = jnp.bfloat16, jnp.float32, jnp.int32
    dma = pltpu.SemaphoreType.DMA
    return pl.pallas_call(
        kernel,
        out_shape=(
            jax.ShapeDtypeStruct((TOK, QW), bf16),
            jax.ShapeDtypeStruct((SLOTS, STEPS, QW), bf16),
        ),
        in_specs=[pl.BlockSpec(memory_space=pl.ANY)] * 15,
        out_specs=(pl.BlockSpec(memory_space=pl.ANY), pl.BlockSpec(memory_space=pl.ANY)),
        scratch_shapes=[
            pltpu.VMEM((NC, ROWS, KC), bf16),
            pltpu.VMEM((NC, KC, W), bf16),
            pltpu.VMEM((ROWS, W), f32),
            pltpu.VMEM((REQ, GROUP * PAGE, HD), bf16),
            pltpu.VMEM((REQ, PAGE, HD), bf16),
            pltpu.VMEM((REQ, PAGE, HD), bf16),
            pltpu.VMEM((PFX + 2 * PAGE, HD), bf16),
            pltpu.VMEM((PFX + 2 * PAGE, 2 * HD), bf16),
            pltpu.VMEM((TOK, QW), bf16),
            pltpu.VMEM((QW,), bf16),
            pltpu.VMEM((HD,), bf16),
            pltpu.VMEM((HD,), bf16),
            pltpu.VMEM((2, ROPE_ROWS, HD), f32),
            pltpu.VMEM((REQ, STEPS, D // NH), bf16),
            pltpu.VMEM((PER, ROWS - TOK, KC), bf16),
            pltpu.VMEM((NS, 2 * PIECE, HD), bf16),
            pltpu.VMEM((NS, 2 * PIECE, HD), bf16),
            pltpu.VMEM((NS, REQ, 2 * PIECE, HD), bf16),
            pltpu.VMEM((NS, REQ, 2 * PIECE, HD), bf16),
            pltpu.VMEM((REQ, GROUP * STEPS, HD), f32),
            pltpu.VMEM((REQ * STEPS, HD), bf16),
            pltpu.VMEM((REQ * STEPS, HD), bf16),
            pltpu.VMEM((REQ * STEPS, HD), bf16),
            pltpu.VMEM((REQ * STEPS, HD), bf16),
            pltpu.VMEM((REQ * STEPS, HD), f32),
            pltpu.VMEM((REQ, GROUP * STEPS, HD), bf16),
            pltpu.VMEM((NS, GROUP * STEPS, HD), bf16),
            pltpu.VMEM((NS, GROUP * STEPS, HD), bf16),
            pltpu.VMEM((SLOTS, STEPS, QW), bf16),
            pltpu.SMEM((64,), i32),
            pltpu.SMEM((64,), i32),
            pltpu.SMEM((64,), i32),
            pltpu.SMEM((128,), i32),
            dma((4, NC)),
            dma((11,)),
            dma((REQ,)),
            dma((NH,)),
            dma((NH,)),
            dma((NS,)),
            dma((NS,)),
            dma((NS,)),
            dma((NS,)),
            dma((NS,)),
            dma((NS,)),
        ],
        compiler_params=pltpu.CompilerParams(
            collective_id=0, has_side_effects=True, vmem_limit_bytes=56 * 1024 * 1024
        ),
        name="layer",
    )(
        tokens,
        w_query,
        w_key,
        w_value,
        b_query,
        b_key,
        b_value,
        prefix_keys.reshape(NS, PIECE, HD),
        prefix_values.reshape(NS, PIECE, HD),
        decode_rows,
        *tables,
        jnp.asarray(rope_table()),
    )


def solution(mesh):
    in_specs = (
        P("seq", None),
        P(None, "head"),
        P(None, "head"),
        P(None, "head"),
        P("head"),
        P("head"),
        P("head"),
        P("seq", None, "head"),
        P("seq", None, "head"),
        P("seq", None, "head"),
        P(),
        P(),
        P(),
        P(),
    )
    out_specs = (P("seq", "head"), P("seq", None, "head"))
    return jax.shard_map(body, mesh=mesh, in_specs=in_specs, out_specs=out_specs, check_vma=False)
```

```python
import functools
import math

import jax
import jax.numpy as jnp
import numpy as np
from jax import lax
from jax.experimental import pallas as pl
from jax.experimental.pallas import tpu as pltpu
from jax.sharding import PartitionSpec as P

HD = 128
PAGE = 128
PFX = 256
STEPS = 4
REQ = 4
SLOTS = 8
NS = 16
NH = 8
GROUP = 8
D = 8192
TOK = REQ * PAGE
DROWS = REQ * STEPS
ROWS = TOK + DROWS
QW = GROUP * HD
W = QW + 2 * HD
FEAT = D // NH
HALF = FEAT // 2
LOOK = 2
PICK_BLOCK = 2
PIECE = PFX // NS
KEYS = PFX + PAGE
ALL_KEYS = KEYS + PAGE
MESH = pl.DeviceIdType.MESH
EXP2_SCALE = math.log2(math.e) / math.sqrt(HD)
ROPE_ROWS = 136


def rope_table():
    frequency = 1000000.0 ** (-np.arange(HD // 2, dtype=np.float64) * 2.0 / HD)
    angles = (PFX + np.arange(ROPE_ROWS, dtype=np.float64))[:, None] * frequency
    cosine = np.concatenate([np.cos(angles), np.cos(angles)], axis=1)
    sine = np.concatenate([-np.sin(angles), np.sin(angles)], axis=1)
    return np.stack([cosine, sine]).astype(np.float32)


def rotate(vectors, cosine, sine):
    return vectors * cosine + pltpu.roll(vectors, HD // 2, 1) * sine


def scores_of(queries, keys):
    return lax.dot_general(queries, keys, (((1,), (1,)), ((), ())), preferred_element_type=jnp.float32)


def softmax_product(score, values_and_ones):
    weight = jnp.exp2((score - jnp.max(score, axis=1, keepdims=True)) * EXP2_SCALE).astype(jnp.bfloat16)
    total = jnp.dot(weight, values_and_ones, preferred_element_type=jnp.float32)
    return total[:, 0:HD] * pltpu.reciprocal(total[:, HD:], approx=True)


def kernel(
    tokens, w_query, w_key, w_value, b_query, b_key, b_value, prefix_keys, prefix_values, decode_rows,
    page_table, prompt_len, soft_ids, plan, rope,
    prompt_res, decode_res,
    x, w, acc, key_all, value_all,
    bq, bk, bv, rope_v, drows, piece, dealt, picked, prefix, dq, dec_f32, dec_res, dec_send, dec_recv,
    table_s, len_s, soft_s, plan_s,
    chunk_sem, small_sem, rows_send, rows_recv, deal_send, deal_recv, pick_send, pick_recv, res_send, res_recv,
):
    s = lax.axis_index("seq")
    h = lax.axis_index("head")

    def piece_copies(n, block, start, length):
        source = pl.multiple_of(lax.rem(h + block, NH) * FEAT + start, length)
        here = pl.ds(pl.multiple_of(block * FEAT + start, length), length)
        at = pl.ds(source, length)
        return (
            pltpu.make_async_copy(tokens.at[:, at], x.at[pl.ds(0, TOK), here], chunk_sem.at[0, n]),
            pltpu.make_async_copy(w_query.at[at, :], w.at[here, pl.ds(0, QW)], chunk_sem.at[1, n]),
            pltpu.make_async_copy(w_key.at[at, :], w.at[here, pl.ds(QW, HD)], chunk_sem.at[2, n]),
            pltpu.make_async_copy(w_value.at[at, :], w.at[here, pl.ds(QW + HD, HD)], chunk_sem.at[3, n]),
        )

    halves = (piece_copies(0, 0, 0, HALF), piece_copies(NH, 0, HALF, HALF))

    def block_copies(b):
        return piece_copies(b, b, 0, FEAT)

    def start(copies):
        for copy in copies:
            copy.start()

    def wait(copies):
        for copy in copies:
            copy.wait()

    small = [
        pltpu.make_async_copy(src, dst, small_sem.at[n])
        for n, (src, dst) in enumerate(
            (
                (decode_rows, drows),
                (prefix_keys, piece.at[:, pl.ds(0, PIECE), :]),
                (prefix_values, piece.at[:, pl.ds(PIECE, PIECE), :]),
                (soft_ids, soft_s),
                (page_table, table_s),
                (prompt_len, len_s),
                (plan, plan_s),
                (b_query, bq),
                (b_key, bk),
                (b_value, bv),
                (rope, rope_v),
            )
        )
    ]

    def over_seq(act):
        def step(k, _):
            act(lax.rem(s + k, NS))
            return 0

        lax.fori_loop(1, NS, step, 0)

    def over_head(act):
        def step(k, _):
            act(k)
            return 0

        lax.fori_loop(1, NH, step, 0)

    def rows_copy(b):
        return pltpu.make_async_remote_copy(
            src_ref=x.at[pl.ds(TOK, DROWS), pl.ds(0, FEAT)],
            dst_ref=x.at[pl.ds(TOK, DROWS), pl.ds(pl.multiple_of(b * FEAT, FEAT), FEAT)],
            send_sem=rows_send.at[b],
            recv_sem=rows_recv.at[b],
            device_id=(s, lax.rem(h + NH - b, NH)),
            device_id_type=MESH,
        )

    def seq_copy(source, target, send, recv):
        def copy(peer, owner):
            return pltpu.make_async_remote_copy(
                src_ref=source.at[peer],
                dst_ref=target.at[owner],
                send_sem=send.at[peer],
                recv_sem=recv.at[owner],
                device_id=(peer, h),
                device_id_type=MESH,
            )

        return copy

    deal_copy = seq_copy(piece, dealt, deal_send, deal_recv)
    pick_copy = seq_copy(picked, prefix, pick_send, pick_recv)
    result_copy = seq_copy(dec_send, dec_recv, res_send, res_recv)

    barrier = pltpu.get_barrier_semaphore()

    def greet(peer):
        pl.semaphore_signal(barrier, inc=1, device_id=peer, device_id_type=MESH)

    over_seq(lambda peer: greet((peer, h)))
    over_head(lambda k: greet((s, lax.rem(h + k, NH))))
    start(small[:3])
    start(halves[0])
    start(halves[1])
    start(small[3:])
    for b in range(1, LOOK):
        start(block_copies(b))

    small[0].wait()
    x[TOK:ROWS, 0:FEAT] = jnp.concatenate([drows[i].astype(jnp.float32) for i in range(REQ)], axis=0).astype(jnp.bfloat16)
    pl.semaphore_wait(barrier, NS - 1 + NH - 1)
    over_head(lambda b: rows_copy(b).start())
    for copy in small[1:3]:
        copy.wait()
    dealt[s] = piece[s]
    over_seq(lambda peer: deal_copy(peer, s).start())

    def pick():
        over_seq(lambda peer: deal_copy(s, peer).wait_recv())

        def one(d, _):
            for j in range(REQ):
                picked[d, j] = dealt[soft_s[REQ * d + j]]
            return 0

        lax.fori_loop(0, NS, one, 0)
        prefix[s] = picked[s]
        over_seq(lambda peer: pick_copy(peer, s).start())

    def project(begin, length, add):
        at = pl.ds(begin, length)
        for n in range(W // 256):
            to = slice(256 * n, 256 * n + 256)
            product = jnp.dot(x[:, at], w[at, to], preferred_element_type=jnp.float32)
            if add:
                acc[:, to] += product
            else:
                acc[:, to] = product

    def project_block(b, _):
        wait(block_copies(b))
        rows_copy(b).wait_recv()

        @pl.when(b + LOOK < NH)
        def _():
            start(block_copies(b + LOOK))

        @pl.when(b == PICK_BLOCK)
        def _():
            pick()

        project(pl.multiple_of(b * FEAT, FEAT), FEAT, True)
        return 0

    wait(halves[0])
    project(0, HALF, False)
    wait(halves[1])
    start(block_copies(LOOK))
    project(HALF, HALF, True)
    wait(small[3:])
    lax.fori_loop(1, NH, project_block, 0)

    b_q = bq[...].astype(jnp.float32).reshape(1, QW)
    b_k = bk[...].astype(jnp.float32).reshape(1, HD)
    b_v = bv[...].astype(jnp.float32).reshape(1, HD)
    cosine = rope_v[0, 0:PAGE, :]
    sine = rope_v[1, 0:PAGE, :]

    holder, length = [], []
    for p in range(REQ):
        who, live = 0, 0
        for i in range(REQ):
            mine = table_s[REQ * s + i] == REQ * s + p
            who += jnp.where(mine, i, 0)
            live += jnp.where(mine, len_s[REQ * s + i], 0)
        holder.append(jnp.minimum(who, REQ - 1))
        length.append(live)

    cosine_d = jnp.concatenate([rope_v[0, pl.ds(len_s[REQ * s + i], STEPS), :] for i in range(REQ)], axis=0)
    sine_d = jnp.concatenate([rope_v[1, pl.ds(len_s[REQ * s + i], STEPS), :] for i in range(REQ)], axis=0)
    for j in range(GROUP):
        at = slice(HD * j, HD * j + HD)
        dec_f32[j, 0:DROWS, :] = rotate(acc[TOK:ROWS, at] + b_q[:, at], cosine_d, sine_d)
        for i in range(REQ):
            dq[i, STEPS * j : STEPS * j + STEPS, :] = dec_f32[j, STEPS * i : STEPS * i + STEPS, :]
    step_keys = rotate(acc[TOK:ROWS, QW : QW + HD] + b_k, cosine_d, sine_d).astype(jnp.bfloat16)
    step_values = (acc[TOK:ROWS, QW + HD : W] + b_v).astype(jnp.bfloat16)
    step_keys = jnp.concatenate([step_keys, jnp.zeros((PAGE - DROWS, HD), jnp.bfloat16)], axis=0)
    step_values = jnp.concatenate([step_values, jnp.zeros((PAGE - DROWS, HD), jnp.bfloat16)], axis=0)

    for p in range(REQ):
        rows = slice(PAGE * p, PAGE * p + PAGE)
        key_all[p, PFX:KEYS, :] = rotate(acc[rows, QW : QW + HD] + b_k, cosine, sine).astype(jnp.bfloat16)
        value_all[p, PFX:KEYS, 0:HD] = (acc[rows, QW + HD : W] + b_v).astype(jnp.bfloat16)
        key_all[p, KEYS:, :] = step_keys
        value_all[p, KEYS:, 0:HD] = step_values
        value_all[p, :, HD:] = jnp.ones((ALL_KEYS, HD), jnp.bfloat16)
    over_seq(lambda peer: pick_copy(s, peer).wait_recv())
    for p in range(REQ):
        key_all[p, 0:PFX, :] = prefix[:, holder[p], 0:PIECE, :].reshape(PFX, HD)
        value_all[p, 0:PFX, 0:HD] = prefix[:, holder[p], PIECE : 2 * PIECE, :].reshape(PFX, HD)

    col = lax.broadcasted_iota(jnp.int32, (GROUP * STEPS, ALL_KEYS), 1)
    step = lax.rem(lax.broadcasted_iota(jnp.int32, (GROUP * STEPS, ALL_KEYS), 0), STEPS)
    for p in range(REQ):
        own = col - (KEYS + STEPS * holder[p])
        live = (col < PFX + length[p]) | ((own >= 0) & (own <= step))
        score = jnp.where(live, scores_of(dq[holder[p]].astype(jnp.bfloat16), key_all[p]), -1e30)
        dec_res[p] = softmax_product(score, value_all[p]).astype(jnp.bfloat16)

    def route(o, _):
        which = 0
        for c in range(SLOTS):
            offset = plan_s[SLOTS * o + c] - REQ * s
            which += jnp.where((offset >= 0) & (offset < REQ), offset, 0)
        page = table_s[REQ * s + jnp.minimum(which, REQ - 1)] - REQ * s
        dec_send[o] = dec_res[jnp.clip(page, 0, REQ - 1)]
        return 0

    lax.fori_loop(0, NS, route, 0)
    dec_recv[s] = dec_send[s]
    over_seq(lambda peer: result_copy(peer, s).start())

    causal = jnp.where(
        lax.broadcasted_iota(jnp.int32, (PAGE, PAGE), 1) <= lax.broadcasted_iota(jnp.int32, (PAGE, PAGE), 0), 0.0, -1e30
    )
    causal = jnp.concatenate([causal] * GROUP, axis=0)
    slot = lax.broadcasted_iota(jnp.int32, (PAGE, HD), 0)
    for p in range(REQ):
        rows = slice(PAGE * p, PAGE * p + PAGE)
        query = jnp.concatenate(
            [
                rotate(acc[rows, HD * j : HD * j + HD] + b_q[:, HD * j : HD * j + HD], cosine, sine).astype(jnp.bfloat16)
                for j in range(GROUP)
            ],
            axis=0,
        )
        score = scores_of(query, key_all[p, 0:KEYS, :])
        score = jnp.concatenate([score[:, 0:PFX], score[:, PFX:] + causal], axis=1)
        result = softmax_product(score, value_all[p, 0:KEYS, :])
        for j in range(GROUP):
            prompt_res[rows, HD * j : HD * j + HD] = jnp.where(
                slot < length[p], result[PAGE * j : PAGE * j + PAGE, :], 0.0
            ).astype(jnp.bfloat16)

    over_seq(lambda peer: result_copy(s, peer).wait_recv())
    for c in range(SLOTS):
        request = plan_s[SLOTS * s + c]
        live = jnp.where(request >= 0, 1.0, 0.0)
        dec_f32[c] = dec_recv[jnp.maximum(request, 0) // REQ].astype(jnp.float32) * live
        decode_res[c] = jnp.concatenate(
            [dec_f32[c, STEPS * j : STEPS * j + STEPS, :] for j in range(GROUP)], axis=1
        ).astype(jnp.bfloat16)

    over_head(lambda b: rows_copy(b).wait_send())
    over_seq(lambda peer: deal_copy(peer, s).wait_send())
    over_seq(lambda peer: pick_copy(peer, s).wait_send())
    over_seq(lambda peer: result_copy(peer, s).wait_send())


def store_kernel(prompt_res, decode_res, prefill_out, decode_out, sem):
    copies = (
        pltpu.make_async_copy(prompt_res, prefill_out, sem.at[0]),
        pltpu.make_async_copy(decode_res, decode_out, sem.at[1]),
    )
    for copy in copies:
        copy.start()
    for copy in copies:
        copy.wait()


def body(*operands):
    (tokens, w_query, w_key, w_value, b_query, b_key, b_value, prefix_keys, prefix_values, decode_rows, *tables) = operands
    bf16, f32, i32 = jnp.bfloat16, jnp.float32, jnp.int32
    dma = pltpu.SemaphoreType.DMA
    anywhere = pl.BlockSpec(memory_space=pl.ANY)
    results = pl.pallas_call(
        kernel,
        out_shape=(pltpu.VMEM((TOK, QW), bf16), pltpu.VMEM((SLOTS, STEPS, QW), bf16)),
        in_specs=[anywhere] * 15,
        scratch_shapes=[
            pltpu.VMEM((ROWS, D), bf16),
            pltpu.VMEM((D, W), bf16),
            pltpu.VMEM((ROWS, W), f32),
            pltpu.VMEM((REQ, ALL_KEYS, HD), bf16),
            pltpu.VMEM((REQ, ALL_KEYS, 2 * HD), bf16),
            pltpu.VMEM((QW,), bf16),
            pltpu.VMEM((HD,), bf16),
            pltpu.VMEM((HD,), bf16),
            pltpu.VMEM((2, ROPE_ROWS, HD), f32),
            pltpu.VMEM((REQ, STEPS, FEAT), bf16),
            pltpu.VMEM((NS, 2 * PIECE, HD), bf16),
            pltpu.VMEM((NS, 2 * PIECE, HD), bf16),
            pltpu.VMEM((NS, REQ, 2 * PIECE, HD), bf16),
            pltpu.VMEM((NS, REQ, 2 * PIECE, HD), bf16),
            pltpu.VMEM((REQ, GROUP * STEPS, HD), f32),
            pltpu.VMEM((GROUP, GROUP * STEPS, HD), f32),
            pltpu.VMEM((REQ, GROUP * STEPS, HD), bf16),
            pltpu.VMEM((NS, GROUP * STEPS, HD), bf16),
            pltpu.VMEM((NS, GROUP * STEPS, HD), bf16),
            pltpu.SMEM((64,), i32),
            pltpu.SMEM((64,), i32),
            pltpu.SMEM((64,), i32),
            pltpu.SMEM((128,), i32),
            dma((4, NH + 1)),
            dma((11,)),
            dma((NH,)),
            dma((NH,)),
            dma((NS,)),
            dma((NS,)),
            dma((NS,)),
            dma((NS,)),
            dma((NS,)),
            dma((NS,)),
        ],
        compiler_params=pltpu.CompilerParams(
            collective_id=0, has_side_effects=True, vmem_limit_bytes=56 * 1024 * 1024
        ),
        name="layer",
    )(
        tokens,
        w_query,
        w_key,
        w_value,
        b_query,
        b_key,
        b_value,
        prefix_keys.reshape(NS, PIECE, HD),
        prefix_values.reshape(NS, PIECE, HD),
        decode_rows,
        *tables,
        jnp.asarray(rope_table()),
    )
    return pl.pallas_call(
        store_kernel,
        out_shape=(jax.ShapeDtypeStruct((TOK, QW), bf16), jax.ShapeDtypeStruct((SLOTS, STEPS, QW), bf16)),
        in_specs=[pl.BlockSpec(memory_space=pltpu.VMEM)] * 2,
        out_specs=(anywhere, anywhere),
        scratch_shapes=[dma((2,))],
        compiler_params=pltpu.CompilerParams(vmem_limit_bytes=8 * 1024 * 1024),
        name="store",
    )(*results)


def solution(mesh):
    in_specs = (
        P("seq", None),
        P(None, "head"),
        P(None, "head"),
        P(None, "head"),
        P("head"),
        P("head"),
        P("head"),
        P("seq", None, "head"),
        P("seq", None, "head"),
        P("seq", None, "head"),
        P(),
        P(),
        P(),
        P(),
    )
    out_specs = (P("seq", "head"), P("seq", None, "head"))
    return jax.shard_map(body, mesh=mesh, in_specs=in_specs, out_specs=out_specs, check_vma=False)
```

```python
import functools
import math

import jax
import jax.numpy as jnp
import numpy as np
from jax import lax
from jax.experimental import pallas as pl
from jax.experimental.pallas import tpu as pltpu
from jax.sharding import PartitionSpec as P

HD = 128
PAGE = 128
PFX = 256
STEPS = 4
REQ = 4
SLOTS = 8
NS = 16
NH = 8
GROUP = 8
D = 8192
TOK = REQ * PAGE
DROWS = REQ * STEPS
ROWS = TOK + DROWS
QW = GROUP * HD
W = QW + 2 * HD
FEAT = D // NH
HALF = FEAT // 2
LOOK = 2
SEND_BLOCK = 1
PICK_BLOCK = 3
EARLY = 768
LATE_DEPTH = 4096
PIECE = PFX // NS
KEYS = PFX + PAGE
ALL_KEYS = KEYS + PAGE
MESH = pl.DeviceIdType.MESH
EXP2_SCALE = math.log2(math.e) / math.sqrt(HD)
ROPE_ROWS = 136


def rope_table():
    frequency = 1000000.0 ** (-np.arange(HD // 2, dtype=np.float64) * 2.0 / HD)
    angles = (PFX + np.arange(ROPE_ROWS, dtype=np.float64))[:, None] * frequency
    cosine = np.concatenate([np.cos(angles), np.cos(angles)], axis=1)
    sine = np.concatenate([-np.sin(angles), np.sin(angles)], axis=1)
    return np.stack([cosine, sine]).astype(np.float32)


def rotate(vectors, cosine, sine):
    return vectors * cosine + pltpu.roll(vectors, HD // 2, 1) * sine


def scores_of(queries, keys):
    return lax.dot_general(queries, keys, (((1,), (1,)), ((), ())), preferred_element_type=jnp.float32)


def softmax_product(score, values_and_ones):
    weight = jnp.exp2((score - jnp.max(score, axis=1, keepdims=True)) * EXP2_SCALE).astype(jnp.bfloat16)
    total = jnp.dot(weight, values_and_ones, preferred_element_type=jnp.float32)
    return total[:, 0:HD] * pltpu.reciprocal(total[:, HD:], approx=True)


def kernel(
    tokens, w_query, w_key, w_value, b_query, b_key, b_value, prefix_keys, prefix_values, decode_rows,
    page_table, prompt_len, soft_ids, plan, rope,
    prompt_res, decode_res,
    x, rows_in, w, acc, key_all, value_all,
    bq, bk, bv, rope_v, drows, piece, dealt, picked, prefix, dq, dec_f32, dec_res, dec_send, dec_recv,
    table_s, len_s, soft_s, plan_s,
    chunk_sem, small_sem, rows_send, rows_recv, deal_send, deal_recv, pick_send, pick_recv, res_send, res_recv,
):
    s = lax.axis_index("seq")
    h = lax.axis_index("head")

    def piece_copies(n, block, start, length):
        source = pl.multiple_of(lax.rem(h + block, NH) * FEAT + start, length)
        here = pl.ds(pl.multiple_of(block * FEAT + start, length), length)
        at = pl.ds(source, length)
        return (
            pltpu.make_async_copy(tokens.at[:, at], x.at[pl.ds(0, TOK), here], chunk_sem.at[0, n]),
            pltpu.make_async_copy(w_query.at[at, :], w.at[here, pl.ds(0, QW)], chunk_sem.at[1, n]),
            pltpu.make_async_copy(w_key.at[at, :], w.at[here, pl.ds(QW, HD)], chunk_sem.at[2, n]),
            pltpu.make_async_copy(w_value.at[at, :], w.at[here, pl.ds(QW + HD, HD)], chunk_sem.at[3, n]),
        )

    halves = (piece_copies(0, 0, 0, HALF), piece_copies(NH, 0, HALF, HALF))

    def block_copies(b):
        return piece_copies(b, b, 0, FEAT)

    def start(copies):
        for copy in copies:
            copy.start()

    def wait(copies):
        for copy in copies:
            copy.wait()

    small = [
        pltpu.make_async_copy(src, dst, small_sem.at[n])
        for n, (src, dst) in enumerate(
            (
                (decode_rows, drows),
                (prefix_keys, piece.at[:, pl.ds(0, PIECE), :]),
                (prefix_values, piece.at[:, pl.ds(PIECE, PIECE), :]),
                (soft_ids, soft_s),
                (page_table, table_s),
                (prompt_len, len_s),
                (plan, plan_s),
                (b_query, bq),
                (b_key, bk),
                (b_value, bv),
                (rope, rope_v),
            )
        )
    ]

    def over_seq(act):
        for k in range(1, NS):
            act(lax.rem(s + k, NS))

    def over_head(act):
        for b in range(1, NH):
            act(b)

    def rows_copy(b):
        return pltpu.make_async_remote_copy(
            src_ref=rows_in.at[:, pl.ds(0, FEAT)],
            dst_ref=rows_in.at[:, pl.ds(pl.multiple_of(b * FEAT, FEAT), FEAT)],
            send_sem=rows_send.at[b],
            recv_sem=rows_recv.at[b],
            device_id=(s, lax.rem(h + NH - b, NH)),
            device_id_type=MESH,
        )

    def seq_copy(source, target, send, recv):
        def copy(peer, owner):
            return pltpu.make_async_remote_copy(
                src_ref=source.at[peer],
                dst_ref=target.at[owner],
                send_sem=send.at[peer],
                recv_sem=recv.at[owner],
                device_id=(peer, h),
                device_id_type=MESH,
            )

        return copy

    deal_copy = seq_copy(piece, dealt, deal_send, deal_recv)
    pick_copy = seq_copy(picked, prefix, pick_send, pick_recv)
    result_copy = seq_copy(dec_send, dec_recv, res_send, res_recv)

    barrier = pltpu.get_barrier_semaphore()

    def greet(peer):
        pl.semaphore_signal(barrier, inc=1, device_id=peer, device_id_type=MESH)

    over_seq(lambda peer: greet((peer, h)))
    over_head(lambda k: greet((s, lax.rem(h + k, NH))))
    start(small[:3])
    start(halves[0])
    start(halves[1])
    start(small[3:])
    for b in range(1, LOOK):
        start(block_copies(b))

    def deal():
        pl.semaphore_wait(barrier, NS - 1 + NH - 1)
        over_head(lambda b: rows_copy(b).start())
        wait(small[1:3])
        dealt[s] = piece[s]
        over_seq(lambda peer: deal_copy(peer, s).start())

    small[0].wait()
    own_rows = jnp.concatenate([drows[i].astype(jnp.float32) for i in range(REQ)], axis=0).astype(jnp.bfloat16)
    rows_in[:, 0:FEAT] = own_rows
    x[TOK:ROWS, 0:FEAT] = own_rows
    x[TOK:ROWS, FEAT : (SEND_BLOCK + 1) * FEAT] = jnp.zeros((DROWS, SEND_BLOCK * FEAT), jnp.bfloat16)

    def pick():
        over_seq(lambda peer: deal_copy(s, peer).wait_recv())

        def one(d, _):
            for j in range(REQ):
                picked[d, j] = dealt[soft_s[REQ * d + j]]
            return 0

        lax.fori_loop(0, NS, one, 0)
        prefix[s] = picked[s]
        over_seq(lambda peer: pick_copy(peer, s).start())

    early = [(n, n + 256) for n in range(0, EARLY, 256)] + [(QW, W)]
    late = [(n, n + 256) for n in range(EARLY, QW, 256)]

    def project(begin, length, add):
        at = pl.ds(begin, length)
        for rows, tiles in ((slice(0, ROWS), early), (slice(TOK, ROWS), late)):
            for left, right in tiles:
                product = jnp.dot(x[rows, at], w[at, left:right], preferred_element_type=jnp.float32)
                if add:
                    acc[rows, left:right] += product
                else:
                    acc[rows, left:right] = product

    def project_block(b, _):
        wait(block_copies(b))

        @pl.when(b + LOOK < NH)
        def _():
            start(block_copies(b + LOOK))

        @pl.when(b == SEND_BLOCK)
        def _():
            deal()

        @pl.when(b == PICK_BLOCK)
        def _():
            pick()

        at = pl.ds(pl.multiple_of(b * FEAT, FEAT), FEAT)

        @pl.when(b > SEND_BLOCK)
        def _():
            rows_copy(b).wait_recv()
            x[TOK:ROWS, at] = rows_in[:, at]

        project(at.start, FEAT, True)
        return 0

    wait(halves[0])
    project(0, HALF, False)
    wait(halves[1])
    start(block_copies(LOOK))
    project(HALF, HALF, True)
    wait(small[3:])
    lax.fori_loop(1, NH, project_block, 0)

    for b in range(1, SEND_BLOCK + 1):
        rows_copy(b).wait_recv()
    behind = slice(FEAT, (SEND_BLOCK + 1) * FEAT)
    for n in range(0, W, 256):
        to = slice(n, n + 256)
        acc[TOK:ROWS, to] += jnp.dot(rows_in[:, behind], w[behind, to], preferred_element_type=jnp.float32)

    b_q = bq[...].astype(jnp.float32).reshape(1, QW)
    b_k = bk[...].astype(jnp.float32).reshape(1, HD)
    b_v = bv[...].astype(jnp.float32).reshape(1, HD)
    cosine = rope_v[0, 0:PAGE, :]
    sine = rope_v[1, 0:PAGE, :]

    holder, length = [], []
    for p in range(REQ):
        who, live = 0, 0
        for i in range(REQ):
            mine = table_s[REQ * s + i] == REQ * s + p
            who += jnp.where(mine, i, 0)
            live += jnp.where(mine, len_s[REQ * s + i], 0)
        holder.append(jnp.minimum(who, REQ - 1))
        length.append(live)

    cosine_d = jnp.concatenate([rope_v[0, pl.ds(len_s[REQ * s + i], STEPS), :] for i in range(REQ)], axis=0)
    sine_d = jnp.concatenate([rope_v[1, pl.ds(len_s[REQ * s + i], STEPS), :] for i in range(REQ)], axis=0)
    for j in range(GROUP):
        at = slice(HD * j, HD * j + HD)
        dec_f32[j, 0:DROWS, :] = rotate(acc[TOK:ROWS, at] + b_q[:, at], cosine_d, sine_d)
        for i in range(REQ):
            dq[i, STEPS * j : STEPS * j + STEPS, :] = dec_f32[j, STEPS * i : STEPS * i + STEPS, :]
    step_keys = rotate(acc[TOK:ROWS, QW : QW + HD] + b_k, cosine_d, sine_d).astype(jnp.bfloat16)
    step_values = (acc[TOK:ROWS, QW + HD : W] + b_v).astype(jnp.bfloat16)
    step_keys = jnp.concatenate([step_keys, jnp.zeros((PAGE - DROWS, HD), jnp.bfloat16)], axis=0)
    step_values = jnp.concatenate([step_values, jnp.zeros((PAGE - DROWS, HD), jnp.bfloat16)], axis=0)

    for p in range(REQ):
        rows = slice(PAGE * p, PAGE * p + PAGE)
        key_all[p, PFX:KEYS, :] = rotate(acc[rows, QW : QW + HD] + b_k, cosine, sine).astype(jnp.bfloat16)
        value_all[p, PFX:KEYS, 0:HD] = (acc[rows, QW + HD : W] + b_v).astype(jnp.bfloat16)
        key_all[p, KEYS:, :] = step_keys
        value_all[p, KEYS:, 0:HD] = step_values
        value_all[p, :, HD:] = jnp.ones((ALL_KEYS, HD), jnp.bfloat16)
    over_seq(lambda peer: pick_copy(s, peer).wait_recv())
    for p in range(REQ):
        key_all[p, 0:PFX, :] = prefix[:, holder[p], 0:PIECE, :].reshape(PFX, HD)
        value_all[p, 0:PFX, 0:HD] = prefix[:, holder[p], PIECE : 2 * PIECE, :].reshape(PFX, HD)

    col = lax.broadcasted_iota(jnp.int32, (GROUP * STEPS, ALL_KEYS), 1)
    step = lax.rem(lax.broadcasted_iota(jnp.int32, (GROUP * STEPS, ALL_KEYS), 0), STEPS)
    for p in range(REQ):
        own = col - (KEYS + STEPS * holder[p])
        live = (col < PFX + length[p]) | ((own >= 0) & (own <= step))
        score = jnp.where(live, scores_of(dq[holder[p]].astype(jnp.bfloat16), key_all[p]), -1e30)
        dec_res[p] = softmax_product(score, value_all[p]).astype(jnp.bfloat16)

    def route(o, _):
        which = 0
        for c in range(SLOTS):
            offset = plan_s[SLOTS * o + c] - REQ * s
            which += jnp.where((offset >= 0) & (offset < REQ), offset, 0)
        page = table_s[REQ * s + jnp.minimum(which, REQ - 1)] - REQ * s
        dec_send[o] = dec_res[jnp.clip(page, 0, REQ - 1)]
        return 0

    lax.fori_loop(0, NS, route, 0)
    dec_recv[s] = dec_send[s]
    over_seq(lambda peer: result_copy(peer, s).start())

    causal = jnp.where(
        lax.broadcasted_iota(jnp.int32, (PAGE, PAGE), 1) <= lax.broadcasted_iota(jnp.int32, (PAGE, PAGE), 0), 0.0, -1e30
    )
    slot = lax.broadcasted_iota(jnp.int32, (PAGE, HD), 0)

    def attend(p, heads):
        rows = slice(PAGE * p, PAGE * p + PAGE)
        query = jnp.concatenate(
            [
                rotate(acc[rows, HD * j : HD * j + HD] + b_q[:, HD * j : HD * j + HD], cosine, sine).astype(jnp.bfloat16)
                for j in heads
            ],
            axis=0,
        )
        score = scores_of(query, key_all[p, 0:KEYS, :])
        own = score[:, PFX:] + jnp.concatenate([causal] * len(heads), axis=0)
        result = softmax_product(jnp.concatenate([score[:, 0:PFX], own], axis=1), value_all[p, 0:KEYS, :])
        for i, j in enumerate(heads):
            prompt_res[rows, HD * j : HD * j + HD] = jnp.where(
                slot < length[p], result[PAGE * i : PAGE * i + PAGE, :], 0.0
            ).astype(jnp.bfloat16)

    acc[0:TOK, EARLY:QW] = jnp.zeros((TOK, QW - EARLY), jnp.float32)

    def project_late(i, _):
        at = pl.ds(pl.multiple_of(i * LATE_DEPTH, LATE_DEPTH), LATE_DEPTH)
        for left, right in late:
            acc[0:TOK, left:right] += jnp.dot(x[0:TOK, at], w[at, left:right], preferred_element_type=jnp.float32)
        return 0

    lax.fori_loop(0, D // LATE_DEPTH, project_late, 0)
    for p in range(REQ):
        attend(p, range(GROUP))

    over_seq(lambda peer: result_copy(s, peer).wait_recv())
    for c in range(SLOTS):
        request = plan_s[SLOTS * s + c]
        live = jnp.where(request >= 0, 1.0, 0.0)
        dec_f32[c] = dec_recv[jnp.maximum(request, 0) // REQ].astype(jnp.float32) * live
        decode_res[c] = jnp.concatenate(
            [dec_f32[c, STEPS * j : STEPS * j + STEPS, :] for j in range(GROUP)], axis=1
        ).astype(jnp.bfloat16)

    over_head(lambda b: rows_copy(b).wait_send())
    over_seq(lambda peer: deal_copy(peer, s).wait_send())
    over_seq(lambda peer: pick_copy(peer, s).wait_send())
    over_seq(lambda peer: result_copy(peer, s).wait_send())


def store_kernel(prompt_res, decode_res, prefill_out, decode_out, sem):
    copies = (
        pltpu.make_async_copy(prompt_res, prefill_out, sem.at[0]),
        pltpu.make_async_copy(decode_res, decode_out, sem.at[1]),
    )
    for copy in copies:
        copy.start()
    for copy in copies:
        copy.wait()


def body(*operands):
    (tokens, w_query, w_key, w_value, b_query, b_key, b_value, prefix_keys, prefix_values, decode_rows, *tables) = operands
    bf16, f32, i32 = jnp.bfloat16, jnp.float32, jnp.int32
    dma = pltpu.SemaphoreType.DMA
    anywhere = pl.BlockSpec(memory_space=pl.ANY)
    results = pl.pallas_call(
        kernel,
        out_shape=(pltpu.VMEM((TOK, QW), bf16), pltpu.VMEM((SLOTS, STEPS, QW), bf16)),
        in_specs=[anywhere] * 15,
        scratch_shapes=[
            pltpu.VMEM((ROWS, D), bf16),
            pltpu.VMEM((DROWS, D), bf16),
            pltpu.VMEM((D, W), bf16),
            pltpu.VMEM((ROWS, W), f32),
            pltpu.VMEM((REQ, ALL_KEYS, HD), bf16),
            pltpu.VMEM((REQ, ALL_KEYS, 2 * HD), bf16),
            pltpu.VMEM((QW,), bf16),
            pltpu.VMEM((HD,), bf16),
            pltpu.VMEM((HD,), bf16),
            pltpu.VMEM((2, ROPE_ROWS, HD), f32),
            pltpu.VMEM((REQ, STEPS, FEAT), bf16),
            pltpu.VMEM((NS, 2 * PIECE, HD), bf16),
            pltpu.VMEM((NS, 2 * PIECE, HD), bf16),
            pltpu.VMEM((NS, REQ, 2 * PIECE, HD), bf16),
            pltpu.VMEM((NS, REQ, 2 * PIECE, HD), bf16),
            pltpu.VMEM((REQ, GROUP * STEPS, HD), f32),
            pltpu.VMEM((GROUP, GROUP * STEPS, HD), f32),
            pltpu.VMEM((REQ, GROUP * STEPS, HD), bf16),
            pltpu.VMEM((NS, GROUP * STEPS, HD), bf16),
            pltpu.VMEM((NS, GROUP * STEPS, HD), bf16),
            pltpu.SMEM((64,), i32),
            pltpu.SMEM((64,), i32),
            pltpu.SMEM((64,), i32),
            pltpu.SMEM((128,), i32),
            dma((4, NH + 1)),
            dma((11,)),
            dma((NH,)),
            dma((NH,)),
            dma((NS,)),
            dma((NS,)),
            dma((NS,)),
            dma((NS,)),
            dma((NS,)),
            dma((NS,)),
        ],
        compiler_params=pltpu.CompilerParams(
            collective_id=0, has_side_effects=True, vmem_limit_bytes=56 * 1024 * 1024
        ),
        name="layer",
    )(
        tokens,
        w_query,
        w_key,
        w_value,
        b_query,
        b_key,
        b_value,
        prefix_keys.reshape(NS, PIECE, HD),
        prefix_values.reshape(NS, PIECE, HD),
        decode_rows,
        *tables,
        jnp.asarray(rope_table()),
    )
    return pl.pallas_call(
        store_kernel,
        out_shape=(jax.ShapeDtypeStruct((TOK, QW), bf16), jax.ShapeDtypeStruct((SLOTS, STEPS, QW), bf16)),
        in_specs=[pl.BlockSpec(memory_space=pltpu.VMEM)] * 2,
        out_specs=(anywhere, anywhere),
        scratch_shapes=[dma((2,))],
        compiler_params=pltpu.CompilerParams(vmem_limit_bytes=8 * 1024 * 1024),
        name="store",
    )(*results)


def solution(mesh):
    in_specs = (
        P("seq", None),
        P(None, "head"),
        P(None, "head"),
        P(None, "head"),
        P("head"),
        P("head"),
        P("head"),
        P("seq", None, "head"),
        P("seq", None, "head"),
        P("seq", None, "head"),
        P(),
        P(),
        P(),
        P(),
    )
    out_specs = (P("seq", "head"), P("seq", None, "head"))
    return jax.shard_map(body, mesh=mesh, in_specs=in_specs, out_specs=out_specs, check_vma=False)
```

```python
import functools
import math

import jax
import jax.numpy as jnp
import numpy as np
from jax import lax
from jax.experimental import pallas as pl
from jax.experimental.pallas import tpu as pltpu
from jax.sharding import PartitionSpec as P

HD = 128
PAGE = 128
PFX = 256
STEPS = 4
REQ = 4
SLOTS = 8
NS = 16
NH = 8
GROUP = 8
D = 8192
TOK = REQ * PAGE
DROWS = REQ * STEPS
ROWS = TOK + DROWS
QW = GROUP * HD
W = QW + 2 * HD
FEAT = D // NH
HALF = FEAT // 2
LOOK = 2
SEND_BLOCK = 1
PICK_BLOCK = 3
EARLY = 768
LATE_DEPTH = 4096
PIECE = PFX // NS
KEYS = PFX + PAGE
ALL_KEYS = KEYS + PAGE
MESH = pl.DeviceIdType.MESH
EXP2_SCALE = math.log2(math.e) / math.sqrt(HD)
ROPE_ROWS = 136


def rope_table():
    frequency = 1000000.0 ** (-np.arange(HD // 2, dtype=np.float64) * 2.0 / HD)
    angles = (PFX + np.arange(ROPE_ROWS, dtype=np.float64))[:, None] * frequency
    cosine = np.concatenate([np.cos(angles), np.cos(angles)], axis=1)
    sine = np.concatenate([-np.sin(angles), np.sin(angles)], axis=1)
    return np.stack([cosine, sine]).astype(np.float32)


def rotate(vectors, cosine, sine):
    return vectors * cosine + pltpu.roll(vectors, HD // 2, 1) * sine


def scores_of(queries, keys):
    return lax.dot_general(queries, keys, (((1,), (1,)), ((), ())), preferred_element_type=jnp.float32)


def softmax_product(score, values_and_ones):
    weight = jnp.exp2((score - jnp.max(score, axis=1, keepdims=True)) * EXP2_SCALE).astype(jnp.bfloat16)
    total = jnp.dot(weight, values_and_ones, preferred_element_type=jnp.float32)
    return total[:, 0:HD] * pltpu.reciprocal(total[:, HD:], approx=True)


def kernel(
    tokens, w_query, w_key, w_value, b_query, b_key, b_value, prefix_keys, prefix_values, decode_rows,
    page_table, prompt_len, soft_ids, plan, rope,
    prompt_res, decode_res,
    x, rows_in, w, acc, key_all, value_all,
    bq, bk, bv, rope_v, drows, piece, dealt, picked, prefix, dq, dec_f32, dec_res, dec_send, dec_recv,
    table_s, len_s, soft_s, plan_s,
    chunk_sem, small_sem, rows_send, rows_recv, deal_send, deal_recv, pick_send, pick_recv, res_send, res_recv,
):
    s = lax.axis_index("seq")
    h = lax.axis_index("head")

    def piece_copies(n, block, start, length):
        source = pl.multiple_of(lax.rem(h + block, NH) * FEAT + start, length)
        here = pl.ds(pl.multiple_of(block * FEAT + start, length), length)
        at = pl.ds(source, length)
        return (
            pltpu.make_async_copy(tokens.at[:, at], x.at[pl.ds(0, TOK), here], chunk_sem.at[0, n]),
            pltpu.make_async_copy(w_query.at[at, :], w.at[here, pl.ds(0, QW)], chunk_sem.at[1, n]),
            pltpu.make_async_copy(w_key.at[at, :], w.at[here, pl.ds(QW, HD)], chunk_sem.at[2, n]),
            pltpu.make_async_copy(w_value.at[at, :], w.at[here, pl.ds(QW + HD, HD)], chunk_sem.at[3, n]),
        )

    halves = (piece_copies(0, 0, 0, HALF), piece_copies(NH, 0, HALF, HALF))

    def block_copies(b):
        return piece_copies(b, b, 0, FEAT)

    def start(copies):
        for copy in copies:
            copy.start()

    def wait(copies):
        for copy in copies:
            copy.wait()

    small = [
        pltpu.make_async_copy(src, dst, small_sem.at[n])
        for n, (src, dst) in enumerate(
            (
                (decode_rows, drows),
                (prefix_keys, piece.at[:, pl.ds(0, PIECE), :]),
                (prefix_values, piece.at[:, pl.ds(PIECE, PIECE), :]),
                (soft_ids, soft_s),
                (page_table, table_s),
                (prompt_len, len_s),
                (plan, plan_s),
                (b_query, bq),
                (b_key, bk),
                (b_value, bv),
                (rope, rope_v),
            )
        )
    ]

    def over_seq(act):
        for k in range(1, NS):
            act(lax.rem(s + k, NS))

    def over_head(act):
        for b in range(1, NH):
            act(b)

    def rows_copy(b):
        return pltpu.make_async_remote_copy(
            src_ref=rows_in.at[:, pl.ds(0, FEAT)],
            dst_ref=rows_in.at[:, pl.ds(pl.multiple_of(b * FEAT, FEAT), FEAT)],
            send_sem=rows_send.at[b],
            recv_sem=rows_recv.at[b],
            device_id=(s, lax.rem(h + NH - b, NH)),
            device_id_type=MESH,
        )

    def seq_copy(source, target, send, recv):
        def copy(peer, owner):
            return pltpu.make_async_remote_copy(
                src_ref=source.at[peer],
                dst_ref=target.at[owner],
                send_sem=send.at[peer],
                recv_sem=recv.at[owner],
                device_id=(peer, h),
                device_id_type=MESH,
            )

        return copy

    deal_copy = seq_copy(piece, dealt, deal_send, deal_recv)
    pick_copy = seq_copy(picked, prefix, pick_send, pick_recv)
    result_copy = seq_copy(dec_send, dec_recv, res_send, res_recv)

    barrier = pltpu.get_barrier_semaphore()

    def greet(peer):
        pl.semaphore_signal(barrier, inc=1, device_id=peer, device_id_type=MESH)

    over_seq(lambda peer: greet((peer, h)))
    over_head(lambda k: greet((s, lax.rem(h + k, NH))))
    start(small[:3])
    start(halves[0])
    start(halves[1])
    start(small[3:])
    for b in range(1, LOOK):
        start(block_copies(b))

    def deal():
        pl.semaphore_wait(barrier, NS - 1 + NH - 1)
        over_head(lambda b: rows_copy(b).start())
        wait(small[1:3])
        dealt[s] = piece[s]
        over_seq(lambda peer: deal_copy(peer, s).start())

    small[0].wait()
    own_rows = jnp.concatenate([drows[i].astype(jnp.float32) for i in range(REQ)], axis=0).astype(jnp.bfloat16)
    rows_in[:, 0:FEAT] = own_rows
    x[TOK:ROWS, 0:FEAT] = own_rows
    x[TOK:ROWS, FEAT : (SEND_BLOCK + 1) * FEAT] = jnp.zeros((DROWS, SEND_BLOCK * FEAT), jnp.bfloat16)

    def pick():
        over_seq(lambda peer: deal_copy(s, peer).wait_recv())

        def one(d, _):
            for j in range(REQ):
                picked[d, j] = dealt[soft_s[REQ * d + j]]
            return 0

        lax.fori_loop(0, NS, one, 0)
        prefix[s] = picked[s]
        over_seq(lambda peer: pick_copy(peer, s).start())

    early = [(n, n + 256) for n in range(0, EARLY, 256)] + [(QW, W)]
    late = [(n, n + 256) for n in range(EARLY, QW, 256)]

    def project(begin, length, add):
        at = pl.ds(begin, length)
        for rows, tiles in ((slice(0, ROWS), early), (slice(TOK, ROWS), late)):
            for left, right in tiles:
                product = jnp.dot(x[rows, at], w[at, left:right], preferred_element_type=jnp.float32)
                if add:
                    acc[rows, left:right] += product
                else:
                    acc[rows, left:right] = product

    def project_block(b, _):
        @pl.when(b + LOOK < NH)
        def _():
            start(block_copies(b + LOOK))

        @pl.when(b == SEND_BLOCK)
        def _():
            deal()

        @pl.when(b == PICK_BLOCK)
        def _():
            pick()

        wait(block_copies(b))
        at = pl.ds(pl.multiple_of(b * FEAT, FEAT), FEAT)

        @pl.when(b > SEND_BLOCK)
        def _():
            rows_copy(b).wait_recv()
            x[TOK:ROWS, at] = rows_in[:, at]

        project(at.start, FEAT, True)
        return 0

    wait(halves[0])
    project(0, HALF, False)
    wait(halves[1])
    start(block_copies(LOOK))
    project(HALF, HALF, True)
    wait(small[3:])
    lax.fori_loop(1, NH, project_block, 0)

    for b in range(1, SEND_BLOCK + 1):
        rows_copy(b).wait_recv()
    behind = slice(FEAT, (SEND_BLOCK + 1) * FEAT)
    for n in range(0, W, 256):
        to = slice(n, n + 256)
        acc[TOK:ROWS, to] += jnp.dot(rows_in[:, behind], w[behind, to], preferred_element_type=jnp.float32)

    b_q = bq[...].astype(jnp.float32).reshape(1, QW)
    b_k = bk[...].astype(jnp.float32).reshape(1, HD)
    b_v = bv[...].astype(jnp.float32).reshape(1, HD)
    cosine = rope_v[0, 0:PAGE, :]
    sine = rope_v[1, 0:PAGE, :]

    holder, length = [], []
    for p in range(REQ):
        who, live = 0, 0
        for i in range(REQ):
            mine = table_s[REQ * s + i] == REQ * s + p
            who += jnp.where(mine, i, 0)
            live += jnp.where(mine, len_s[REQ * s + i], 0)
        holder.append(jnp.minimum(who, REQ - 1))
        length.append(live)

    cosine_d = jnp.concatenate([rope_v[0, pl.ds(len_s[REQ * s + i], STEPS), :] for i in range(REQ)], axis=0)
    sine_d = jnp.concatenate([rope_v[1, pl.ds(len_s[REQ * s + i], STEPS), :] for i in range(REQ)], axis=0)
    for j in range(GROUP):
        at = slice(HD * j, HD * j + HD)
        dec_f32[j, 0:DROWS, :] = rotate(acc[TOK:ROWS, at] + b_q[:, at], cosine_d, sine_d)
        for i in range(REQ):
            dq[i, STEPS * j : STEPS * j + STEPS, :] = dec_f32[j, STEPS * i : STEPS * i + STEPS, :]
    step_keys = rotate(acc[TOK:ROWS, QW : QW + HD] + b_k, cosine_d, sine_d).astype(jnp.bfloat16)
    step_values = (acc[TOK:ROWS, QW + HD : W] + b_v).astype(jnp.bfloat16)
    step_keys = jnp.concatenate([step_keys, jnp.zeros((PAGE - DROWS, HD), jnp.bfloat16)], axis=0)
    step_values = jnp.concatenate([step_values, jnp.zeros((PAGE - DROWS, HD), jnp.bfloat16)], axis=0)

    for p in range(REQ):
        rows = slice(PAGE * p, PAGE * p + PAGE)
        key_all[p, PFX:KEYS, :] = rotate(acc[rows, QW : QW + HD] + b_k, cosine, sine).astype(jnp.bfloat16)
        value_all[p, PFX:KEYS, 0:HD] = (acc[rows, QW + HD : W] + b_v).astype(jnp.bfloat16)
        key_all[p, KEYS:, :] = step_keys
        value_all[p, KEYS:, 0:HD] = step_values
        value_all[p, :, HD:] = jnp.ones((ALL_KEYS, HD), jnp.bfloat16)
    over_seq(lambda peer: pick_copy(s, peer).wait_recv())
    for p in range(REQ):
        key_all[p, 0:PFX, :] = prefix[:, holder[p], 0:PIECE, :].reshape(PFX, HD)
        value_all[p, 0:PFX, 0:HD] = prefix[:, holder[p], PIECE : 2 * PIECE, :].reshape(PFX, HD)

    col = lax.broadcasted_iota(jnp.int32, (GROUP * STEPS, ALL_KEYS), 1)
    step = lax.rem(lax.broadcasted_iota(jnp.int32, (GROUP * STEPS, ALL_KEYS), 0), STEPS)
    for p in range(REQ):
        own = col - (KEYS + STEPS * holder[p])
        live = (col < PFX + length[p]) | ((own >= 0) & (own <= step))
        score = jnp.where(live, scores_of(dq[holder[p]].astype(jnp.bfloat16), key_all[p]), -1e30)
        dec_res[p] = softmax_product(score, value_all[p]).astype(jnp.bfloat16)

    def route(o, _):
        which = 0
        for c in range(SLOTS):
            offset = plan_s[SLOTS * o + c] - REQ * s
            which += jnp.where((offset >= 0) & (offset < REQ), offset, 0)
        page = table_s[REQ * s + jnp.minimum(which, REQ - 1)] - REQ * s
        dec_send[o] = dec_res[jnp.clip(page, 0, REQ - 1)]
        return 0

    lax.fori_loop(0, NS, route, 0)
    dec_recv[s] = dec_send[s]
    over_seq(lambda peer: result_copy(peer, s).start())

    causal = jnp.where(
        lax.broadcasted_iota(jnp.int32, (PAGE, PAGE), 1) <= lax.broadcasted_iota(jnp.int32, (PAGE, PAGE), 0), 0.0, -1e30
    )
    slot = lax.broadcasted_iota(jnp.int32, (PAGE, HD), 0)

    def attend(p, heads):
        rows = slice(PAGE * p, PAGE * p + PAGE)
        query = jnp.concatenate(
            [
                rotate(acc[rows, HD * j : HD * j + HD] + b_q[:, HD * j : HD * j + HD], cosine, sine).astype(jnp.bfloat16)
                for j in heads
            ],
            axis=0,
        )
        score = scores_of(query, key_all[p, 0:KEYS, :])
        own = score[:, PFX:] + jnp.concatenate([causal] * len(heads), axis=0)
        result = softmax_product(jnp.concatenate([score[:, 0:PFX], own], axis=1), value_all[p, 0:KEYS, :])
        for i, j in enumerate(heads):
            prompt_res[rows, HD * j : HD * j + HD] = jnp.where(
                slot < length[p], result[PAGE * i : PAGE * i + PAGE, :], 0.0
            ).astype(jnp.bfloat16)

    acc[0:TOK, EARLY:QW] = jnp.zeros((TOK, QW - EARLY), jnp.float32)

    def project_late(i, _):
        at = pl.ds(pl.multiple_of(i * LATE_DEPTH, LATE_DEPTH), LATE_DEPTH)
        for left, right in late:
            acc[0:TOK, left:right] += jnp.dot(x[0:TOK, at], w[at, left:right], preferred_element_type=jnp.float32)
        return 0

    lax.fori_loop(0, D // LATE_DEPTH, project_late, 0)
    for p in range(REQ):
        attend(p, range(GROUP))

    over_seq(lambda peer: result_copy(s, peer).wait_recv())
    for c in range(SLOTS):
        request = plan_s[SLOTS * s + c]
        live = jnp.where(request >= 0, 1.0, 0.0)
        dec_f32[c] = dec_recv[jnp.maximum(request, 0) // REQ].astype(jnp.float32) * live
        decode_res[c] = jnp.concatenate(
            [dec_f32[c, STEPS * j : STEPS * j + STEPS, :] for j in range(GROUP)], axis=1
        ).astype(jnp.bfloat16)

    over_head(lambda b: rows_copy(b).wait_send())
    over_seq(lambda peer: deal_copy(peer, s).wait_send())
    over_seq(lambda peer: pick_copy(peer, s).wait_send())
    over_seq(lambda peer: result_copy(peer, s).wait_send())


def store_kernel(prompt_res, decode_res, prefill_out, decode_out, sem):
    copies = (
        pltpu.make_async_copy(prompt_res, prefill_out, sem.at[0]),
        pltpu.make_async_copy(decode_res, decode_out, sem.at[1]),
    )
    for copy in copies:
        copy.start()
    for copy in copies:
        copy.wait()


def body(*operands):
    (tokens, w_query, w_key, w_value, b_query, b_key, b_value, prefix_keys, prefix_values, decode_rows, *tables) = operands
    bf16, f32, i32 = jnp.bfloat16, jnp.float32, jnp.int32
    dma = pltpu.SemaphoreType.DMA
    anywhere = pl.BlockSpec(memory_space=pl.ANY)
    results = pl.pallas_call(
        kernel,
        out_shape=(pltpu.VMEM((TOK, QW), bf16), pltpu.VMEM((SLOTS, STEPS, QW), bf16)),
        in_specs=[anywhere] * 15,
        scratch_shapes=[
            pltpu.VMEM((ROWS, D), bf16),
            pltpu.VMEM((DROWS, D), bf16),
            pltpu.VMEM((D, W), bf16),
            pltpu.VMEM((ROWS, W), f32),
            pltpu.VMEM((REQ, ALL_KEYS, HD), bf16),
            pltpu.VMEM((REQ, ALL_KEYS, 2 * HD), bf16),
            pltpu.VMEM((QW,), bf16),
            pltpu.VMEM((HD,), bf16),
            pltpu.VMEM((HD,), bf16),
            pltpu.VMEM((2, ROPE_ROWS, HD), f32),
            pltpu.VMEM((REQ, STEPS, FEAT), bf16),
            pltpu.VMEM((NS, 2 * PIECE, HD), bf16),
            pltpu.VMEM((NS, 2 * PIECE, HD), bf16),
            pltpu.VMEM((NS, REQ, 2 * PIECE, HD), bf16),
            pltpu.VMEM((NS, REQ, 2 * PIECE, HD), bf16),
            pltpu.VMEM((REQ, GROUP * STEPS, HD), f32),
            pltpu.VMEM((GROUP, GROUP * STEPS, HD), f32),
            pltpu.VMEM((REQ, GROUP * STEPS, HD), bf16),
            pltpu.VMEM((NS, GROUP * STEPS, HD), bf16),
            pltpu.VMEM((NS, GROUP * STEPS, HD), bf16),
            pltpu.SMEM((64,), i32),
            pltpu.SMEM((64,), i32),
            pltpu.SMEM((64,), i32),
            pltpu.SMEM((128,), i32),
            dma((4, NH + 1)),
            dma((11,)),
            dma((NH,)),
            dma((NH,)),
            dma((NS,)),
            dma((NS,)),
            dma((NS,)),
            dma((NS,)),
            dma((NS,)),
            dma((NS,)),
        ],
        compiler_params=pltpu.CompilerParams(
            collective_id=0, has_side_effects=True, vmem_limit_bytes=56 * 1024 * 1024
        ),
        name="layer",
    )(
        tokens,
        w_query,
        w_key,
        w_value,
        b_query,
        b_key,
        b_value,
        prefix_keys.reshape(NS, PIECE, HD),
        prefix_values.reshape(NS, PIECE, HD),
        decode_rows,
        *tables,
        jnp.asarray(rope_table()),
    )
    return pl.pallas_call(
        store_kernel,
        out_shape=(jax.ShapeDtypeStruct((TOK, QW), bf16), jax.ShapeDtypeStruct((SLOTS, STEPS, QW), bf16)),
        in_specs=[pl.BlockSpec(memory_space=pltpu.VMEM)] * 2,
        out_specs=(anywhere, anywhere),
        scratch_shapes=[dma((2,))],
        compiler_params=pltpu.CompilerParams(vmem_limit_bytes=8 * 1024 * 1024),
        name="store",
    )(*results)


def solution(mesh):
    in_specs = (
        P("seq", None),
        P(None, "head"),
        P(None, "head"),
        P(None, "head"),
        P("head"),
        P("head"),
        P("head"),
        P("seq", None, "head"),
        P("seq", None, "head"),
        P("seq", None, "head"),
        P(),
        P(),
        P(),
        P(),
    )
    out_specs = (P("seq", "head"), P("seq", None, "head"))
    return jax.shard_map(body, mesh=mesh, in_specs=in_specs, out_specs=out_specs, check_vma=False)
```
